32 devices in a mesh: dp: 2 (over core), expert: 4 (over z), tpin: 2 (over y), tpout: 2 (over x).
Axes of the slice: x: 2, y: 2, z: 4, core: 2. Of those that a mesh axis runs over, the one named last changes fastest.
Arguments:
- tokens: bfloat16 [64, 6144], P('expert', ('dp', 'tpin', 'tpout')), may hold values from -6 to 6
- cotangent: bfloat16 [64, 6144], P('expert', ('dp', 'tpin', 'tpout')), may hold values from -6 to 6
- expert_ids: int32 [64, 2], P('expert'), may hold values from 0 to 7, all different within a row; in each aligned block of 16 rows (0 to 15, 16 to 31, ...) at most 6 rows name the same one
- gate_weights: float32 [64, 2], P('expert'), may hold values from 0.25 to 1
- w_gate: bfloat16 [6144, 65536], P(('dp', 'tpin'), ('expert', 'tpout')), may hold values from -0.078125 to 0.078125
- w_up: bfloat16 [6144, 65536], P(('dp', 'tpin'), ('expert', 'tpout')), may hold values from -0.078125 to 0.078125
- w_down: bfloat16 [65536, 6144], P(('expert', 'tpout'), ('dp', 'tpin')), may hold values from -0.0625 to 0.0625
Outputs:
- layer_out: bfloat16 [64, 6144], P('expert', ('dp', 'tpin', 'tpout'))
- token_grad: bfloat16 [64, 6144], P('expert', ('dp', 'tpin', 'tpout'))
- down_grad: bfloat16 [65536, 6144], P(('expert', 'tpout'), ('dp', 'tpin'))
The draws below stay inside these ranges and needn't reach their ends.
Inputs may be any that keep to these rules, and one draw needn't show every extreme that they name: `expert_ids`: each row names 2 different experts. In each aligned block of 16 rows no expert is named by more than 6 rows, a bound that some block reaches.
All inputs are finite; a program needn't handle non-finite values.
Results may differ from the reference program's by a relative error of at most 0.0057.
Values may be sent and summed in bfloat16 or wider, within the bound.
No kernel may reach another device: no remote copies, remote signals or barrier semaphores. Data moves between devices by JAX's collectives and lax.ppermute only.
A program may use at most 192 MiB of HBM per device.

```python
import math
import jax
import jax.numpy as jnp
import numpy as np
from jax import lax

D = 6144
EXPERTS = 8
HID = 8192
TOP = 2
TOK_G = 16
CAP = 6
TOKENS = 64
N_EXPERT = 4


def levels(own_key, dims, split, smallest, largest):
    factor_of, own = 1.0, jax.random.fold_in(own_key, 6)
    for dim, blocks in split:
        steps = jnp.exp(jax.random.uniform(jax.random.fold_in(own, dim), (blocks,), jnp.float32, smallest / len(split), largest / len(split)))
        factor_of = factor_of * jnp.repeat(steps, dims[dim] // blocks).reshape([-1 if axis == dim else 1 for axis in range(len(dims))])
    return factor_of


def shared_out(own_key, own, number, rows, amount, top, reach, skew):
    order = jax.random.permutation(own_key, amount)
    heavy_load, usual = portions_of(amount, rows * top, reach, skew, True), portions_of(amount, rows * top, reach, skew, False)
    places = jnp.arange(amount)

    def named(tallies, rotation):
        used = int((tallies > 0).sum())
        fixed = max(1, used // 4)
        moved = fixed + (places - fixed + rotation * (used - fixed)) % max(1, amount - fixed)
        return jnp.zeros((amount,), jnp.int32).at[order[jnp.where(places < fixed, places, moved)]].set(jnp.asarray(tallies, jnp.int32))

    tallies = jnp.where(number % 4 == 0, named(heavy_load, number // 4), named(usual, number - number // 4 - 1))
    mixed = jax.random.permutation(jax.random.fold_in(own, 3), amount)
    giver, taker = mixed[0:amount // 2 * 2:2], mixed[1:amount // 2 * 2:2]
    room = jnp.minimum(tallies[giver] - 1, reach - tallies[taker]) // 2
    room = jnp.where((giver == order[0]) | (taker == order[0]) | (tallies[taker] == 0), 0, jnp.maximum(room, 0))
    moved = jax.random.randint(jax.random.fold_in(own, 4), (amount // 2,), 0, 1 << 20) % (room + 1)
    tallies = tallies.at[giver].add(-moved).at[taker].add(moved)
    members = jnp.searchsorted(jnp.cumsum(tallies), jnp.arange(rows * top), side="right").astype(jnp.int32)
    grid = members.reshape(top, rows).T
    grid = grid[jax.random.permutation(jax.random.fold_in(own, 1), rows)]
    rotation = jax.random.randint(jax.random.fold_in(own, 2), (rows, 1), 0, top)
    return jnp.take_along_axis(grid, (jnp.arange(top)[None, :] + rotation) % top, axis=1)


def portions_of(number_of, total, bound, slope, full):
    portions = [(1 << 20) // math.isqrt(grade ** slope) + 1 for grade in range(1, number_of + 1)]
    largest = bound if full else min(bound, max(-(-total // number_of), total * portions[0] // sum(portions)))
    least = 1 if total - largest >= number_of - 1 else 0
    counts, surplus = [largest] + [least] * (number_of - 1), total - largest - least * (number_of - 1)
    while surplus > 0:
        candidates = [i for i in range(1, number_of) if counts[i] < largest] or [i for i in range(1, number_of) if counts[i] < bound]
        pool, budget = sum([portions[i] for i in candidates]), surplus
        for i in candidates:
            addition = min(bound - counts[i], max(1, budget * portions[i] // pool), surplus)
            counts[i] = counts[i] + addition
            surplus = surplus - addition
    return np.array(counts)


def scatter_about(rng, shape, deviation, most, cuts=(), kind=jnp.bfloat16):
    loudness = levels(rng, shape, cuts, -0.22, 0.18) if cuts else 1.0
    drawn = jax.random.normal(rng, shape, jnp.float32) * deviation * loudness
    return jnp.minimum(jnp.maximum(drawn, -most), most).astype(kind)


def setup_inputs(seed: int = 0) -> dict:
    keys = jax.random.split(jax.random.key(seed), 8)
    tokens = scatter_about(keys[0], (TOKENS, D), 1.0, 6.0, ((0, 4), (1, 8)))
    cotangent = scatter_about(keys[1], (TOKENS, D), 1.0, 6.0, ((0, 4), (1, 8)))
    expert_ids_keys = jax.random.split(jax.random.fold_in(keys[2], 1), TOKENS // TOK_G)
    expert_ids_turns = jax.random.permutation(jax.random.fold_in(keys[2], 3), TOKENS // TOK_G)
    expert_ids = jax.vmap(lambda own, number: shared_out(jax.random.fold_in(keys[2], 2), own, number, TOK_G, EXPERTS, TOP, CAP, 1))(expert_ids_keys, expert_ids_turns).reshape((TOKENS, TOP))
    gate_weights = jnp.clip(0.25 + 0.75 * jax.random.uniform(keys[3], (TOKENS, TOP), jnp.float32) ** levels(keys[3], (TOKENS, TOP), ((0, 4),), -0.2, 0.2), 0.25, 1.0)
    w_gate = scatter_about(keys[4], (D, EXPERTS * HID), D ** -0.5, 0.078125, ((0, 4), (1, 8)))
    w_up = scatter_about(keys[5], (D, EXPERTS * HID), D ** -0.5, 0.078125, ((0, 4), (1, 8)))
    w_down = scatter_about(keys[6], (EXPERTS * HID, D), HID ** -0.5, 0.0625, ((0, 8), (1, 4)))
    return {"tokens": tokens, "cotangent": cotangent, "expert_ids": expert_ids, "gate_weights": gate_weights, "w_gate": w_gate, "w_up": w_up, "w_down": w_down}


def reference(tokens, cotangent, expert_ids, gate_weights, w_gate, w_up, w_down):
    route_rows = N_EXPERT * CAP
    model_width = tokens.shape[1]

    def expert_step(carry, expert):
        out_acc, grad_acc = carry
        hit = expert_ids == expert
        weight = jnp.sum(jnp.where(hit, gate_weights, jnp.zeros_like(gate_weights)), axis=1)
        routed = jnp.any(hit, axis=1)
        order = jnp.argsort(jnp.logical_not(routed).astype(jnp.int32), stable=True)[:route_rows].astype(jnp.int32)
        x_rows = tokens[order]
        weight_rows = weight[order]
        start = (expert * HID).astype(jnp.int32)
        gate_cols = lax.dynamic_slice_in_dim(w_gate, start, HID, 1)
        up_cols = lax.dynamic_slice_in_dim(w_up, start, HID, 1)
        down_rows = lax.dynamic_slice_in_dim(w_down, start, HID, 0)
        gate = jnp.dot(x_rows, gate_cols, preferred_element_type=jnp.float32)
        up = jnp.dot(x_rows, up_cols, preferred_element_type=jnp.float32)
        sig = jax.nn.sigmoid(gate)
        hidden = (gate * sig * up).astype(jnp.bfloat16)
        expert_out = jnp.dot(hidden, down_rows, preferred_element_type=jnp.float32)
        out_acc = out_acc.at[order].add(weight_rows[:, None] * expert_out)
        routed_grad = (weight_rows[:, None] * cotangent[order].astype(jnp.float32)).astype(jnp.bfloat16)
        hidden_grad = jnp.dot(routed_grad, down_rows.T, preferred_element_type=jnp.float32)
        gate_grad = (hidden_grad * up * sig * (1.0 + gate * (1.0 - sig))).astype(jnp.bfloat16)
        up_grad = (hidden_grad * gate * sig).astype(jnp.bfloat16)
        row_grad = jnp.dot(gate_grad, gate_cols.T, preferred_element_type=jnp.float32) + jnp.dot(up_grad, up_cols.T, preferred_element_type=jnp.float32)
        grad_acc = grad_acc.at[order].add(row_grad)
        down_part = jnp.dot(hidden.T, routed_grad, preferred_element_type=jnp.float32).astype(jnp.bfloat16)
        return (out_acc, grad_acc), down_part

    start_acc = jnp.zeros((tokens.shape[0], model_width), jnp.float32)
    (out_acc, grad_acc), down_parts = lax.scan(expert_step, (start_acc, start_acc), jnp.arange(EXPERTS, dtype=jnp.int32))
    down_grad = down_parts.reshape(EXPERTS * HID, model_width)
    return out_acc.astype(jnp.bfloat16), grad_acc.astype(jnp.bfloat16), down_grad
```

```python
import math

import jax
import jax.numpy as jnp
import numpy as np
from jax import lax
from jax.experimental import pallas as pl
from jax.experimental.pallas import tpu as pltpu
from jax.sharding import PartitionSpec as P

EXPERTS = 8
HID = 8192
CAP = 6
SLAB = 16
ROUTE_AXES = ("tpout", "expert")

NN = (((1,), (0,)), ((), ()))
NT = (((1,), (1,)), ((), ()))
TN = (((0,), (0,)), ((), ()))
VMEM = pl.BlockSpec(memory_space=pltpu.VMEM)
ANY = pl.BlockSpec(memory_space=pl.ANY)


def dot(left, right, dims=NN, precision=None):
    return lax.dot_general(
        left, right, dims, preferred_element_type=jnp.float32, precision=precision
    )


def params():
    return pltpu.CompilerParams(vmem_limit_bytes=44 << 20)


def cost(flops, nbytes):
    return pl.CostEstimate(flops=int(flops), bytes_accessed=int(nbytes), transcendentals=0)


def route_rows(tokens, cotangent, expert_ids, gate_weights, dest_expert):
    tok_rows, feat = tokens.shape
    rows = len(dest_expert) * SLAB
    j = np.arange(rows) % SLAB
    slot = np.where(j < 2 * CAP, j % CAP, -1)
    table = np.stack([np.repeat(np.asarray(dest_expert), SLAB), slot, (j < CAP) * 1, j * 0], 1)
    first = np.zeros((2, rows, expert_ids.shape[1]), np.float32)
    first[0, :, 0] = 1
    first[1, :, 1] = 1
    before = np.triu(np.ones((tok_rows, tok_rows), np.float32), 1)

    def kernel(tok, cot, ids, gw, tab, one, bef, send, home):
        want = tab[:, 0:1].astype(jnp.float32)
        slot = tab[:, 1:2].astype(jnp.float32)
        is_x = tab[:, 2:3] == 1
        fid = ids[...].astype(jnp.float32)
        hit = jnp.zeros((rows, tok_rows), jnp.bool_)
        weight = jnp.zeros((rows, tok_rows), jnp.float32)
        for k in range(2):
            same = dot(one[k], fid, NT) == want
            hit = hit | same
            weight += jnp.where(same, dot(one[k], gw[...], NT, lax.Precision.HIGHEST), 0.0)
        rank = dot(hit.astype(jnp.float32), bef[...])
        chosen = jnp.where(hit & (rank == slot), 1.0, 0.0)
        pick = chosen.astype(jnp.bfloat16)
        row_weight = jnp.sum(chosen * weight, axis=1, keepdims=True)
        x = dot(pick, tok[...])
        dy = row_weight * dot(pick, cot[...])
        send[...] = jnp.where(is_x, x, dy).astype(jnp.bfloat16)
        home[...] = jnp.where(is_x, chosen * weight, chosen)

    return pl.pallas_call(
        kernel,
        in_specs=[VMEM] * 7,
        out_specs=[VMEM] * 2,
        out_shape=[
            jax.ShapeDtypeStruct((rows, feat), jnp.bfloat16),
            jax.ShapeDtypeStruct((rows, tok_rows), jnp.float32),
        ],
        compiler_params=params(),
        name="route_rows",
    )(
        tokens,
        cotangent,
        expert_ids,
        gate_weights,
        jnp.asarray(table, jnp.int32),
        jnp.asarray(first),
        jnp.asarray(before),
    )


def combine_rows(back, home, tok_rows):
    rows, feat = back.shape

    def kernel(b, h, out, grad):
        j = lax.broadcasted_iota(jnp.int32, h.shape, 0) % SLAB
        vals = b[...].astype(jnp.float32)
        for_out = jnp.where(j < CAP, h[...], 0.0)
        for_grad = jnp.where(j < CAP, 0.0, h[...])
        out[...] = dot(for_out, vals, TN, lax.Precision.HIGHEST).astype(jnp.bfloat16)
        grad[...] = dot(for_grad.astype(jnp.bfloat16), b[...], TN).astype(jnp.bfloat16)

    shape = jax.ShapeDtypeStruct((tok_rows, feat), jnp.bfloat16)
    return pl.pallas_call(
        kernel,
        in_specs=[VMEM] * 2,
        out_specs=[VMEM] * 2,
        out_shape=[shape, shape],
        compiler_params=params(),
        name="combine_rows",
    )(back, home)


class Stream:
    def __init__(self, sources, slots, sems, base, width, steps):
        self.sources, self.slots, self.sems = sources, slots, sems
        self.base, self.width, self.steps = base, width, steps
        self.depth = slots[0].shape[0]

    def copies(self, step):
        at = pl.ds(self.base + step * self.width, self.width)
        slot = step % self.depth
        gate, up, down = self.sources
        views = (gate.at[:, at], up.at[:, at], down.at[at, :])
        return [
            pltpu.make_async_copy(view, held.at[slot], self.sems.at[i, slot])
            for i, (view, held) in enumerate(zip(views, self.slots))
        ]

    def open(self):
        for step in range(min(self.depth, self.steps)):
            for copy in self.copies(step):
                copy.start()

    def take(self, step):
        for copy in self.copies(step):
            copy.wait()
        return [held.at[step % self.depth] for held in self.slots]

    def done(self, step):
        if step + self.depth < self.steps:
            for copy in self.copies(step + self.depth):
                copy.start()


def stream_scratch(wide, width, depth):
    return [
        pltpu.VMEM((depth, wide, width), jnp.bfloat16),
        pltpu.VMEM((depth, wide, width), jnp.bfloat16),
        pltpu.VMEM((depth, width, wide), jnp.bfloat16),
        pltpu.SemaphoreType.DMA((3, depth)),
    ]


def block_width(cols):
    width = min(512, cols)
    depth = min(4, cols // width)
    return width, depth


def spread(recv_rows, expert_count, outer_count, x_all, dy_all, recv):
    feat = recv.shape[1]
    slabs = expert_count * SLAB
    r = lax.broadcasted_iota(jnp.int32, (recv_rows, slabs), 0)
    c = lax.broadcasted_iota(jnp.int32, (recv_rows, slabs), 1)
    place = (r // CAP) * SLAB + r % CAP
    for_x = jnp.where(c == place, 1.0, 0.0).astype(jnp.bfloat16)
    for_dy = jnp.where(c == place + CAP, 1.0, 0.0).astype(jnp.bfloat16)
    for o in range(outer_count):
        part = recv[o * slabs : (o + 1) * slabs, :]
        x_all[:, o * feat : (o + 1) * feat] = dot(for_x, part).astype(jnp.bfloat16)
        dy_all[:, o * feat : (o + 1) * feat] = dot(for_dy, part).astype(jnp.bfloat16)


def first_phase(rows_in, w_gate, w_up, w_down, base, cols, counts):
    wide = w_gate.shape[0]
    rows = counts[0] * CAP
    width, depth = block_width(cols)
    steps = cols // width
    opening = len(rows_in) == 1

    def kernel(*refs):
        refs = list(refs)
        rows_refs = [refs.pop(0) for _ in rows_in]
        sources = [refs.pop(0) for _ in range(3)]
        if opening:
            exact, rounded, x_all, dy_all = refs[:4]
            refs = refs[4:]
        else:
            exact, rounded = refs[:2]
            refs = refs[2:]
            x_all, dy_all = rows_refs
        stream = Stream(sources, refs[:3], refs[3], base, width, steps)
        stream.open()
        if opening:
            spread(rows, counts[0], counts[1], x_all, dy_all, rows_refs[0])
        for step in range(steps):
            gate, up, down = stream.take(step)
            at = step * width
            parts = (
                dot(x_all[...], gate[...]),
                dot(x_all[...], up[...]),
                dot(dy_all[...], down[...], NT),
            )
            for i, part in enumerate(parts):
                exact[:, i * cols + at : i * cols + at + width] = part
                rounded[:, i * cols + at : i * cols + at + width] = part.astype(jnp.bfloat16)
            stream.done(step)

    shapes = [
        jax.ShapeDtypeStruct((rows, 3 * cols), jnp.float32),
        jax.ShapeDtypeStruct((rows, 3 * cols), jnp.bfloat16),
    ]
    if opening:
        shapes += [jax.ShapeDtypeStruct((rows, wide), jnp.bfloat16)] * 2
    return pl.pallas_call(
        kernel,
        in_specs=[VMEM] * len(rows_in) + [ANY] * 3,
        out_specs=[VMEM] * len(shapes),
        out_shape=shapes,
        scratch_shapes=stream_scratch(wide, width, depth),
        compiler_params=params(),
        cost_estimate=cost(6 * 256 * wide * cols, 6 * wide * cols),
        name="first_phase",
    )(*rows_in, w_gate, w_up, w_down)


def second_phase(parts, sums, w_gate, w_up, w_down, base, cols, counts, last):
    wide = w_gate.shape[0]
    rows = counts[0] * CAP
    feat = wide // counts[1]
    slabs = counts[0] * SLAB
    width, depth = block_width(cols)
    steps = cols // width

    def kernel(*refs):
        refs = list(refs)
        part_refs = [refs.pop(0) for _ in parts]
        sum_refs = [refs.pop(0) for _ in sums]
        sources = [refs.pop(0) for _ in range(3)]
        hidden = refs.pop(0)
        outs = [refs.pop(0) for _ in range(1 if last else 2)]
        slots, sems = refs[:3], refs[3]
        gate_grad, up_grad = refs[4:6]
        acc = refs[6:8] if last else outs
        stream = Stream(sources, slots, sems, base, width, steps)
        stream.open()
        for step in range(steps):
            at = step * width
            gate, up, hidden_grad = [
                sum(p[:, i * cols + at : i * cols + at + width] for p in part_refs)
                for i in range(3)
            ]
            sig = 1.0 / (1.0 + jnp.exp(-gate))
            act = gate * sig
            here = slice(at, at + width)
            hidden[:, here] = (act * up).astype(jnp.bfloat16)
            gate_grad[:, here] = (
                hidden_grad * up * sig * (1.0 + gate * (1.0 - sig))
            ).astype(jnp.bfloat16)
            up_grad[:, here] = (hidden_grad * act).astype(jnp.bfloat16)
        for step in range(steps):
            w_g, w_u, w_d = stream.take(step)
            here = slice(step * width, (step + 1) * width)
            out = dot(hidden[:, here], w_d[...])
            grad = dot(gate_grad[:, here], w_g[...], NT) + dot(up_grad[:, here], w_u[...], NT)
            if step == 0 and not sums:
                acc[0][...] = out
                acc[1][...] = grad
            elif step == 0:
                acc[0][...] = sum_refs[0][...] + out
                acc[1][...] = sum_refs[1][...] + grad
            else:
                acc[0][...] += out
                acc[1][...] += grad
            stream.done(step)
        if last:
            r = lax.broadcasted_iota(jnp.int32, (slabs, rows), 0)
            c = lax.broadcasted_iota(jnp.int32, (slabs, rows), 1)
            place = (c // CAP) * SLAB + c % CAP
            from_out = jnp.where(r == place, 1.0, 0.0).astype(jnp.bfloat16)
            from_grad = jnp.where(r == place + CAP, 1.0, 0.0).astype(jnp.bfloat16)
            out16 = acc[0][...].astype(jnp.bfloat16)
            grad16 = acc[1][...].astype(jnp.bfloat16)
            for o in range(counts[1]):
                cut = slice(o * feat, (o + 1) * feat)
                outs[0][o * slabs : (o + 1) * slabs, :] = (
                    dot(from_out, out16[:, cut]) + dot(from_grad, grad16[:, cut])
                ).astype(jnp.bfloat16)

    scratch = stream_scratch(wide, width, depth)
    scratch += [pltpu.VMEM((rows, cols), jnp.bfloat16)] * 2
    shapes = [jax.ShapeDtypeStruct((rows, cols), jnp.bfloat16)]
    if last:
        scratch += [pltpu.VMEM((rows, wide), jnp.float32)] * 2
        shapes += [jax.ShapeDtypeStruct((counts[1] * slabs, feat), jnp.bfloat16)]
    else:
        shapes += [jax.ShapeDtypeStruct((rows, wide), jnp.float32)] * 2
    return pl.pallas_call(
        kernel,
        in_specs=[VMEM] * (len(parts) + len(sums)) + [ANY] * 3,
        out_specs=[VMEM] * len(shapes),
        out_shape=shapes,
        scratch_shapes=scratch,
        compiler_params=params(),
        cost_estimate=cost(6 * 256 * wide * cols, 6 * wide * cols),
        name="second_phase",
    )(*parts, *sums, w_gate, w_up, w_down)


def outer_products(hiddens, dy_all):
    rows, wide = dy_all.shape
    cols = hiddens[0].shape[1]
    width = min(512, cols)
    per = cols // width
    total = per * len(hiddens)
    depth = min(4, total)

    def kernel(*refs):
        hidden_refs, (dy, out, held, sems) = refs[: len(hiddens)], refs[len(hiddens) :]

        def copy(step):
            return pltpu.make_async_copy(
                held.at[step % depth], out.at[pl.ds(step * width, width), :], sems.at[step % depth]
            )

        for step in range(total):
            if step >= depth:
                copy(step - depth).wait()
            at = (step % per) * width
            block = hidden_refs[step // per][:, at : at + width]
            held[step % depth] = dot(block, dy[...], TN).astype(jnp.bfloat16)
            copy(step).start()
        for step in range(total - depth, total):
            copy(step).wait()

    return pl.pallas_call(
        kernel,
        in_specs=[VMEM] * (len(hiddens) + 1),
        out_specs=ANY,
        out_shape=jax.ShapeDtypeStruct((cols * len(hiddens), wide), jnp.bfloat16),
        scratch_shapes=[
            pltpu.VMEM((depth, width, wide), jnp.bfloat16),
            pltpu.SemaphoreType.DMA((depth,)),
        ],
        compiler_params=params(),
        cost_estimate=cost(2 * 256 * wide * cols * len(hiddens), 2 * wide * cols * len(hiddens)),
        name="outer_products",
    )(*hiddens, dy_all)


def from_peers(value, axis):
    size = lax.axis_size(axis)
    return [
        lax.ppermute(value, axis, [(i, (i + hop) % size) for i in range(size)])
        for hop in range(1, size)
    ]


def per_device(tokens, cotangent, expert_ids, gate_weights, w_gate, w_up, w_down):
    expert_count = lax.axis_size("expert")
    outer_count = lax.axis_size("tpout")
    counts = (expert_count, outer_count)
    tok_rows, feat = tokens.shape
    unit_cols = w_gate.shape[1]
    dest_expert = [
        (i * outer_count + o) * unit_cols // HID
        for o in range(outer_count)
        for i in range(expert_count)
    ]
    send, home = route_rows(tokens, cotangent, expert_ids, gate_weights, dest_expert)

    def exchange(rows):
        cut = rows.reshape(outer_count * expert_count, SLAB, feat)
        return lax.all_to_all(cut, ROUTE_AXES, 0, 0, tiled=True).reshape(rows.shape)

    rows_in = (exchange(send),)
    chunks = 2 if unit_cols % 1024 == 0 else 1
    cols = unit_cols // chunks
    firsts = []
    for chunk in range(chunks):
        exact, rounded, *opened = first_phase(
            rows_in, w_gate, w_up, w_down, chunk * cols, cols, counts
        )
        if opened:
            rows_in = tuple(opened)
        firsts.append((exact, from_peers(rounded, "tpin")))
    dy_all = rows_in[1]
    sums, hiddens = (), []
    for chunk, (exact, others) in enumerate(firsts):
        mine = exact + sum(o.astype(jnp.float32) for o in others)
        parts = [mine] + from_peers(mine, "dp")
        last = chunk == chunks - 1
        hidden, *sums = second_phase(
            parts, sums, w_gate, w_up, w_down, chunk * cols, cols, counts, last
        )
        hiddens.append(hidden)
    back = exchange(sums[0])
    down_grad = outer_products(hiddens, dy_all)
    layer_out, token_grad = combine_rows(back, home, tok_rows)
    return layer_out, token_grad, down_grad


def solution(mesh):
    wide = P("expert", ("dp", "tpin", "tpout"))
    rows = P("expert", None)
    into = P(("dp", "tpin"), ("expert", "tpout"))
    out_of = P(("expert", "tpout"), ("dp", "tpin"))
    return jax.shard_map(
        per_device,
        mesh=mesh,
        in_specs=(wide, wide, rows, rows, into, into, out_of),
        out_specs=(wide, wide, out_of),
        check_vma=False,
    )
```

```python
import jax
import jax.numpy as jnp
from jax import lax
from jax.experimental import pallas as pl
from jax.experimental.pallas import tpu as pltpu
from jax.sharding import PartitionSpec as P

EXPERTS = 8
HID = 8192
CAP = 6
KEEP_BLOCKS = 4
SLAB = 16
ROUTE_AXES = ("expert", "tpout")

NN = (((1,), (0,)), ((), ()))
NT = (((1,), (1,)), ((), ()))
TN = (((0,), (0,)), ((), ()))
VMEM = pl.BlockSpec(memory_space=pltpu.VMEM)
ANY = pl.BlockSpec(memory_space=pltpu.HBM)


def dot(left, right, dims=NN, precision=None):
    return lax.dot_general(
        left, right, dims, preferred_element_type=jnp.float32, precision=precision
    )


def params():
    return pltpu.CompilerParams(vmem_limit_bytes=32 << 20)


def cost(flops, nbytes):
    return pl.CostEstimate(flops=int(flops), bytes_accessed=int(nbytes), transcendentals=0)


def route_rows(tokens, cotangent, ids, weights, devices, unit_cols):
    tok_rows, feat = tokens.shape
    rows = devices * SLAB
    top = ids.shape[0]

    def kernel(tok_hbm, cot_hbm, ids_hbm, gw_hbm, send, home, tok, cot, ids_v, gw_v, sems):
        pairs = ((ids_hbm, ids_v), (gw_hbm, gw_v), (tok_hbm, tok), (cot_hbm, cot))
        copies = [
            pltpu.make_async_copy(src, dst, sems.at[i]) for i, (src, dst) in enumerate(pairs)
        ]
        for copy in copies:
            copy.start()
        row = lax.broadcasted_iota(jnp.int32, (rows, tok_rows), 0)
        j = row % SLAB
        want = row // SLAB * unit_cols // HID
        slot = jnp.where(j < 2 * CAP, j % CAP, -1)
        is_x = j < CAP
        earlier = lax.broadcasted_iota(jnp.int32, (tok_rows, tok_rows), 0)
        later = lax.broadcasted_iota(jnp.int32, (tok_rows, tok_rows), 1)
        before = jnp.where(earlier < later, 1.0, 0.0)
        copies[0].wait()
        copies[1].wait()
        hit = jnp.zeros((rows, tok_rows), jnp.float32)
        weight = jnp.zeros((rows, tok_rows), jnp.float32)
        for k in range(top):
            same = ids_v[k : k + 1, :] == want
            hit += jnp.where(same, 1.0, 0.0)
            weight += jnp.where(same, gw_v[k : k + 1, :], 0.0)
        rank = dot(hit, before)
        chosen = jnp.where(rank == slot.astype(jnp.float32), hit, 0.0)
        pick = chosen.astype(jnp.bfloat16)
        row_weight = jnp.sum(chosen * weight, axis=1, keepdims=True)
        home[...] = jnp.where(is_x, chosen * weight, chosen)
        copies[2].wait()
        x = dot(pick, tok[...])
        copies[3].wait()
        dy = row_weight * dot(pick, cot[...])
        send[...] = jnp.where(is_x[:, 0:1], x, dy).astype(jnp.bfloat16)

    return pl.pallas_call(
        kernel,
        in_specs=[ANY] * 4,
        out_specs=[VMEM] * 2,
        out_shape=[
            jax.ShapeDtypeStruct((rows, feat), jnp.bfloat16),
            jax.ShapeDtypeStruct((rows, tok_rows), jnp.float32),
        ],
        scratch_shapes=[
            pltpu.VMEM(tokens.shape, tokens.dtype),
            pltpu.VMEM(cotangent.shape, cotangent.dtype),
            pltpu.VMEM(ids.shape, ids.dtype),
            pltpu.VMEM(weights.shape, weights.dtype),
            pltpu.SemaphoreType.DMA((4,)),
        ],
        compiler_params=pltpu.CompilerParams(vmem_limit_bytes=63 << 20),
        name="route_rows",
    )(tokens, cotangent, ids, weights)


def combine_rows(back, home, tok_rows):
    rows, feat = back.shape

    def kernel(b, h, out, grad):
        j = lax.broadcasted_iota(jnp.int32, h.shape, 0) % SLAB
        vals = b[...].astype(jnp.float32)
        for_out = jnp.where(j < CAP, h[...], 0.0)
        for_grad = jnp.where(j < CAP, 0.0, h[...])
        out[...] = dot(for_out, vals, TN, lax.Precision.HIGHEST).astype(jnp.bfloat16)
        grad[...] = dot(for_grad.astype(jnp.bfloat16), b[...], TN).astype(jnp.bfloat16)

    shape = jax.ShapeDtypeStruct((tok_rows, feat), jnp.bfloat16)
    return pl.pallas_call(
        kernel,
        in_specs=[VMEM] * 2,
        out_specs=[VMEM] * 2,
        out_shape=[shape, shape],
        compiler_params=params(),
        name="combine_rows",
    )(back, home)


class Stream:
    def __init__(self, sources, slots, sems, base, width, steps, kept, present):
        self.sources, self.slots, self.sems = sources, slots, sems
        self.base, self.width, self.steps = base, width, steps
        self.kept, self.present = kept, present
        self.room = kept.shape[1] // width
        self.depth = slots[0].shape[0]

    def place(self, which, step):
        if which == 0 and step < self.room:
            return self.kept.at[:, pl.ds(step * self.width, self.width)]
        return self.slots[which].at[step % self.depth]

    def copy(self, which, step):
        if self.present and which == 0 and step < self.room:
            return None
        at = pl.ds(self.base + step * self.width, self.width)
        source = self.sources[which]
        return pltpu.make_async_copy(
            source.at[at, :] if which == 2 else source.at[:, at],
            self.place(which, step),
            self.sems.at[which, step % self.depth],
        )

    def start(self, which, step):
        copy = self.copy(which, step) if step < self.steps else None
        if copy is not None:
            copy.start()

    def open(self):
        for step in range(self.depth):
            for which in range(3):
                self.start(which, step)

    def take(self, which, step):
        copy = self.copy(which, step)
        if copy is not None:
            copy.wait()
        return self.place(which, step)

    def done(self, which, step):
        self.start(which, step + self.depth)


def stream_scratch(wide, width, depth):
    return [
        pltpu.VMEM((depth, wide, width), jnp.bfloat16),
        pltpu.VMEM((depth, wide, width), jnp.bfloat16),
        pltpu.VMEM((depth, width, wide), jnp.bfloat16),
        pltpu.SemaphoreType.DMA((3, depth)),
    ]


def block_width(cols):
    width = min(512, cols)
    depth = min(4, cols // width)
    return width, depth


def slab_rows(shape, slot_dim, part, outer, counts):
    slot = lax.broadcasted_iota(jnp.int32, shape, slot_dim)
    row = lax.broadcasted_iota(jnp.int32, shape, 1 - slot_dim)
    device = slot // CAP * counts[1] + outer
    place = device * SLAB + part * CAP + slot % CAP
    return jnp.where(row == place, 1.0, 0.0).astype(jnp.bfloat16)


def spread(recv, x_all, dy_all, counts):
    feat = recv.shape[1]
    for outer in range(counts[1]):
        for part, whole in enumerate((x_all, dy_all)):
            pick = slab_rows((whole.shape[0], recv.shape[0]), 0, part, outer, counts)
            whole[:, outer * feat : (outer + 1) * feat] = dot(pick, recv[...]).astype(jnp.bfloat16)


def first_phase(rows_in, w_gate, w_up, w_down, base, cols, counts):
    wide = w_gate.shape[0]
    rows = counts[0] * CAP
    width, depth = block_width(cols)
    steps = cols // width
    keep = min(KEEP_BLOCKS, steps) * width
    opening = len(rows_in) == 1

    def kernel(*refs):
        refs = list(refs)
        rows_refs = [refs.pop(0) for _ in rows_in]
        sources = [refs.pop(0) for _ in range(3)]
        exact, rounded, kept, *refs = refs
        x_all, dy_all = refs[:2] if opening else rows_refs
        *slots, sems = refs[-4:]
        stream = Stream(sources, slots, sems, base, width, steps, kept, False)
        stream.open()
        if opening:
            spread(rows_refs[0], x_all, dy_all, counts)
        for step in range(steps):
            at = step * width
            for i in range(3):
                weight = stream.take(i, step)[...]
                if i < 2:
                    part = dot(x_all[...], weight)
                else:
                    part = dot(dy_all[...], weight, NT)
                here = slice(i * cols + at, i * cols + at + width)
                exact[:, here] = part
                rounded[:, here] = part.astype(jnp.bfloat16)
                stream.done(i, step)

    shapes = [
        jax.ShapeDtypeStruct((rows, 3 * cols), jnp.float32),
        jax.ShapeDtypeStruct((rows, 3 * cols), jnp.bfloat16),
        jax.ShapeDtypeStruct((wide, keep), jnp.bfloat16),
    ]
    if opening:
        shapes += [jax.ShapeDtypeStruct((rows, wide), jnp.bfloat16)] * 2
    return pl.pallas_call(
        kernel,
        in_specs=[VMEM] * len(rows_in) + [ANY] * 3,
        out_specs=[VMEM] * len(shapes),
        out_shape=shapes,
        scratch_shapes=stream_scratch(wide, width, depth),
        compiler_params=params(),
        cost_estimate=cost(6 * 256 * wide * cols, 6 * wide * cols),
        name="first_phase",
    )(*rows_in, w_gate, w_up, w_down)


def second_phase(parts, sums, held, w_gate, w_up, w_down, base, cols, counts, last):
    wide = w_gate.shape[0]
    rows = counts[0] * CAP
    feat = wide // counts[1]
    slabs = counts[0] * counts[1] * SLAB
    width, depth = block_width(cols)
    steps = cols // width

    def kernel(*refs):
        refs = list(refs)
        part_refs = [refs.pop(0) for _ in parts]
        sum_refs = [refs.pop(0) for _ in sums]
        kept = refs.pop(0)
        sources = [refs.pop(0) for _ in range(3)]
        hidden = refs.pop(0)
        outs = [refs.pop(0) for _ in range(1 if last else 2)]
        slots, sems, gate_grad, up_grad = refs[:3], refs[3], refs[4], refs[5]
        acc = refs[6:8] if last else outs
        stream = Stream(sources, slots, sems, base, width, steps, kept, True)
        stream.open()
        for step in range(steps):
            at = step * width
            gate, up, hidden_grad = [
                sum(p[:, i * cols + at : i * cols + at + width].astype(jnp.float32) for p in part_refs)
                for i in range(3)
            ]
            sig = 1.0 / (1.0 + jnp.exp(-gate))
            act = gate * sig
            here = slice(at, at + width)
            hidden[:, here] = (act * up).astype(jnp.bfloat16)
            gate_grad[:, here] = (
                hidden_grad * up * sig * (1.0 + gate * (1.0 - sig))
            ).astype(jnp.bfloat16)
            up_grad[:, here] = (hidden_grad * act).astype(jnp.bfloat16)
        for step in range(steps):
            at = step * width
            here = slice(at, at + width)
            for i, left in enumerate((gate_grad, up_grad, hidden)):
                weight = stream.take(i, step)[...]
                part = dot(left[:, here], weight, NN if i == 2 else NT)
                total = acc[0] if i == 2 else acc[1]
                if step > 0 or i == 1:
                    total[...] += part
                elif sums:
                    total[...] = sum_refs[0 if i == 2 else 1][...] + part
                else:
                    total[...] = part
                stream.done(i, step)
        if last:
            out16 = acc[0][...].astype(jnp.bfloat16)
            grad16 = acc[1][...].astype(jnp.bfloat16)
            packed = []
            for outer in range(counts[1]):
                cut = slice(outer * feat, (outer + 1) * feat)
                picks = [slab_rows((slabs, rows), 1, part, outer, counts) for part in range(2)]
                packed.append(dot(picks[0], out16[:, cut]) + dot(picks[1], grad16[:, cut]))
            outs[0][...] = sum(packed).astype(jnp.bfloat16)

    scratch = stream_scratch(wide, width, depth)
    scratch += [pltpu.VMEM((rows, cols), jnp.bfloat16)] * 2
    shapes = [jax.ShapeDtypeStruct((rows, cols), jnp.bfloat16)]
    if last:
        scratch += [pltpu.VMEM((rows, wide), jnp.float32)] * 2
        shapes += [jax.ShapeDtypeStruct((slabs, feat), jnp.bfloat16)]
    else:
        shapes += [jax.ShapeDtypeStruct((rows, wide), jnp.float32)] * 2
    return pl.pallas_call(
        kernel,
        in_specs=[VMEM] * (len(parts) + len(sums) + 1) + [ANY] * 3,
        out_specs=[VMEM] * len(shapes),
        out_shape=shapes,
        scratch_shapes=scratch,
        compiler_params=params(),
        cost_estimate=cost(6 * 256 * wide * cols, 6 * wide * cols),
        name="second_phase",
    )(*parts, *sums, held, w_gate, w_up, w_down)


def outer_products(hidden, dy_all, chunk, chunks, earlier):
    rows, wide = dy_all.shape
    cols = hidden.shape[1]
    width = min(512, cols)
    total = cols // width
    depth = min(4, total)

    def kernel(*refs):
        hid, dy = refs[:2]
        out, held, sems = refs[-3:]

        def copy(step):
            at = pl.ds(chunk * cols + step * width, width)
            slot = step % depth
            return pltpu.make_async_copy(held.at[slot], out.at[at, :], sems.at[slot])

        for step in range(total):
            if step >= depth:
                copy(step - depth).wait()
            block = hid[:, step * width : (step + 1) * width]
            held[step % depth] = dot(block, dy[...], TN).astype(jnp.bfloat16)
            copy(step).start()
        for step in range(total - depth, total):
            copy(step).wait()

    return pl.pallas_call(
        kernel,
        in_specs=[VMEM] * 2 + [ANY] * len(earlier),
        out_specs=ANY,
        out_shape=jax.ShapeDtypeStruct((cols * chunks, wide), jnp.bfloat16),
        input_output_aliases={2: 0} if earlier else {},
        scratch_shapes=[
            pltpu.VMEM((depth, width, wide), jnp.bfloat16),
            pltpu.SemaphoreType.DMA((depth,)),
        ],
        compiler_params=params(),
        cost_estimate=cost(2 * 256 * wide * cols, 2 * wide * cols),
        name="outer_products",
    )(hidden, dy_all, *earlier)


def from_peers(value, axis):
    size = lax.axis_size(axis)
    return [
        lax.ppermute(value, axis, [(i, (i + hop) % size) for i in range(size)])
        for hop in range(1, size)
    ]


def per_device(tokens, cotangent, expert_ids, gate_weights, w_gate, w_up, w_down):
    expert_count = lax.axis_size("expert")
    outer_count = lax.axis_size("tpout")
    counts = (expert_count, outer_count)
    tok_rows, feat = tokens.shape
    unit_cols = w_gate.shape[1]
    send, home = route_rows(
        tokens, cotangent, expert_ids.T, gate_weights.T, expert_count * outer_count, unit_cols
    )

    def exchange(rows):
        cut = rows.reshape(expert_count * outer_count, SLAB, feat)
        return lax.all_to_all(cut, ROUTE_AXES, 0, 0, tiled=True).reshape(rows.shape)

    rows_in = (exchange(send),)
    chunks = 2 if unit_cols % 1024 == 0 else 1
    cols = unit_cols // chunks
    firsts = []
    for chunk in range(chunks):
        exact, rounded, kept, *opened = first_phase(
            rows_in, w_gate, w_up, w_down, chunk * cols, cols, counts
        )
        if opened:
            rows_in = tuple(opened)
        firsts.append([exact, from_peers(rounded, "tpin"), kept])
        if chunk > 0:
            pair = lax.optimization_barrier((firsts[chunk - 1][0], exact))
            firsts[chunk - 1][0], firsts[chunk][0] = pair
    dy_all = rows_in[1]
    sums, hiddens, down_grad = (), [], ()
    for chunk, (exact, others, kept) in enumerate(firsts):
        if hiddens:
            down_grad = (outer_products(hiddens[-1], dy_all, chunk - 1, chunks, down_grad),)
            exact, sums, down_grad = lax.optimization_barrier((exact, tuple(sums), down_grad))
        mine = exact + sum(o.astype(jnp.float32) for o in others)
        parts = [mine] + from_peers(mine.astype(jnp.bfloat16), "dp")
        last = chunk == chunks - 1
        hidden, *sums = second_phase(
            parts, sums, kept, w_gate, w_up, w_down, chunk * cols, cols, counts, last
        )
        hiddens.append(hidden)
    back = exchange(sums[0])
    down_grad = outer_products(hiddens[-1], dy_all, chunks - 1, chunks, down_grad)
    layer_out, token_grad = combine_rows(back, home, tok_rows)
    return layer_out, token_grad, down_grad


def solution(mesh):
    wide = P("expert", ("dp", "tpin", "tpout"))
    rows = P("expert", None)
    into = P(("dp", "tpin"), ("expert", "tpout"))
    out_of = P(("expert", "tpout"), ("dp", "tpin"))
    return jax.shard_map(
        per_device,
        mesh=mesh,
        in_specs=(wide, wide, rows, rows, into, into, out_of),
        out_specs=(wide, wide, out_of),
        check_vma=False,
    )
```

```python
import jax
import jax.numpy as jnp
from jax import lax
from jax.experimental import pallas as pl
from jax.experimental.pallas import tpu as pltpu
from jax.sharding import PartitionSpec as P

EXPERTS = 8
HID = 8192
CAP = 6
BLOCK = 512
DEPTH = 4
KEEP_BLOCKS = 4
FIRST_SHARE = 16
EARLY_BLOCKS = 3
SLAB = 16
ROUTE_AXES = ("expert", "tpout")

NN = (((1,), (0,)), ((), ()))
NT = (((1,), (1,)), ((), ()))
TN = (((0,), (0,)), ((), ()))
VMEM = pl.BlockSpec(memory_space=pltpu.VMEM)
ANY = pl.BlockSpec(memory_space=pltpu.HBM)


def dot(left, right, dims=NN, precision=None):
    return lax.dot_general(
        left, right, dims, preferred_element_type=jnp.float32, precision=precision
    )


def params(mib=16):
    return pltpu.CompilerParams(vmem_limit_bytes=mib << 20)


def cost(flops, nbytes):
    return pl.CostEstimate(flops=int(flops), bytes_accessed=int(nbytes), transcendentals=0)


def route_rows(tokens, cotangent, ids, weights, devices, unit_cols):
    tok_rows, feat = tokens.shape
    rows = devices * SLAB
    top = ids.shape[0]

    def kernel(tok_hbm, cot_hbm, ids_hbm, gw_hbm, send, home, tok, cot, ids_v, gw_v, sems):
        pairs = ((ids_hbm, ids_v), (gw_hbm, gw_v), (tok_hbm, tok), (cot_hbm, cot))
        copies = [
            pltpu.make_async_copy(src, dst, sems.at[i]) for i, (src, dst) in enumerate(pairs)
        ]
        for copy in copies:
            copy.start()
        row = lax.broadcasted_iota(jnp.int32, (rows, tok_rows), 0)
        j = row % SLAB
        want = row // SLAB * unit_cols // HID
        slot = jnp.where(j < 2 * CAP, j % CAP, -1)
        is_x = j < CAP
        earlier = lax.broadcasted_iota(jnp.int32, (tok_rows, tok_rows), 0)
        later = lax.broadcasted_iota(jnp.int32, (tok_rows, tok_rows), 1)
        before = jnp.where(earlier < later, 1.0, 0.0)
        copies[0].wait()
        copies[1].wait()
        hit = jnp.zeros((rows, tok_rows), jnp.float32)
        weight = jnp.zeros((rows, tok_rows), jnp.float32)
        for k in range(top):
            same = ids_v[k : k + 1, :] == want
            hit += jnp.where(same, 1.0, 0.0)
            weight += jnp.where(same, gw_v[k : k + 1, :], 0.0)
        rank = dot(hit, before)
        chosen = jnp.where(rank == slot.astype(jnp.float32), hit, 0.0)
        pick = chosen.astype(jnp.bfloat16)
        row_weight = jnp.sum(chosen * weight, axis=1, keepdims=True)
        home[...] = jnp.where(is_x, chosen * weight, chosen)
        copies[2].wait()
        x = dot(pick, tok[...])
        copies[3].wait()
        dy = row_weight * dot(pick, cot[...])
        send[...] = jnp.where(is_x[:, 0:1], x, dy).astype(jnp.bfloat16)

    return pl.pallas_call(
        kernel,
        in_specs=[ANY] * 4,
        out_specs=[VMEM] * 2,
        out_shape=[
            jax.ShapeDtypeStruct((rows, feat), jnp.bfloat16),
            jax.ShapeDtypeStruct((rows, tok_rows), jnp.float32),
        ],
        scratch_shapes=[
            pltpu.VMEM(tokens.shape, tokens.dtype),
            pltpu.VMEM(cotangent.shape, cotangent.dtype),
            pltpu.VMEM(ids.shape, ids.dtype),
            pltpu.VMEM(weights.shape, weights.dtype),
            pltpu.SemaphoreType.DMA((4,)),
        ],
        compiler_params=params(63),
        name="route_rows",
    )(tokens, cotangent, ids, weights)


def combine_rows(back, home, tok_rows):
    rows, feat = back.shape

    def kernel(b, h, out, grad):
        j = lax.broadcasted_iota(jnp.int32, h.shape, 0) % SLAB
        vals = b[...].astype(jnp.float32)
        for_out = jnp.where(j < CAP, h[...], 0.0)
        for_grad = jnp.where(j < CAP, 0.0, h[...])
        out[...] = dot(for_out, vals, TN, lax.Precision.HIGHEST).astype(jnp.bfloat16)
        grad[...] = dot(for_grad.astype(jnp.bfloat16), b[...], TN).astype(jnp.bfloat16)

    shape = jax.ShapeDtypeStruct((tok_rows, feat), jnp.bfloat16)
    return pl.pallas_call(
        kernel,
        in_specs=[VMEM] * 2,
        out_specs=[VMEM] * 2,
        out_shape=[shape, shape],
        compiler_params=params(),
        name="combine_rows",
    )(back, home)


def block_list(cols):
    return [(at, min(BLOCK, cols - at)) for at in range(0, cols, BLOCK)]


class Stream:
    def __init__(self, sources, slots, sems, base, blocks, stays):
        self.sources, self.slots, self.sems = sources, slots, sems
        self.base, self.blocks, self.stays = base, blocks, stays

    def place(self, which, step):
        at, width = self.blocks[step]
        ref, count, offset, _ = self.stays.get(which, (None, 0, 0, False))
        if step < count:
            return ref.at[:, pl.ds(offset + at, width)]
        slot = self.slots[which].at[step % DEPTH]
        if width == BLOCK:
            return slot
        return slot.at[pl.ds(0, width), :] if which == 2 else slot.at[:, pl.ds(0, width)]

    def copy(self, which, step):
        _, count, _, present = self.stays.get(which, (None, 0, 0, False))
        if present and step < count:
            return None
        at, width = self.blocks[step]
        at = pl.ds(self.base + at, width)
        source = self.sources[which]
        return pltpu.make_async_copy(
            source.at[at, :] if which == 2 else source.at[:, at],
            self.place(which, step),
            self.sems.at[which, step % DEPTH],
        )

    def start(self, which, step):
        copy = self.copy(which, step) if step < len(self.blocks) else None
        if copy is not None:
            copy.start()

    def open(self):
        for step in range(DEPTH):
            for which in range(3):
                self.start(which, step)

    def take(self, which, step):
        copy = self.copy(which, step)
        if copy is not None:
            copy.wait()
        return self.place(which, step)

    def done(self, which, step):
        self.start(which, step + DEPTH)


def stream_scratch(wide, weights):
    slots = [
        pltpu.VMEM((DEPTH, BLOCK, wide) if which == 2 else (DEPTH, wide, BLOCK), jnp.bfloat16)
        for which in weights
    ]
    return slots + [pltpu.SemaphoreType.DMA((3, DEPTH))]


def slab_rows(shape, slot_dim, part, outer, counts):
    slot = lax.broadcasted_iota(jnp.int32, shape, slot_dim)
    row = lax.broadcasted_iota(jnp.int32, shape, 1 - slot_dim)
    device = slot // CAP * counts[1] + outer
    place = device * SLAB + part * CAP + slot % CAP
    return jnp.where(row == place, 1.0, 0.0).astype(jnp.bfloat16)


def spread(recv, x_all, dy_all, counts):
    feat = recv.shape[1]
    for outer in range(counts[1]):
        for part, whole in enumerate((x_all, dy_all)):
            pick = slab_rows((whole.shape[0], recv.shape[0]), 0, part, outer, counts)
            whole[:, outer * feat : (outer + 1) * feat] = dot(pick, recv[...]).astype(jnp.bfloat16)


def streamed(held, blocks):
    return [i for i in range(3) if i not in held or held[i][2] < len(blocks)]


def first_phase(rows_in, weights, held, saves, base, cols, counts):
    wide = weights[0].shape[0]
    rows = counts[0] * CAP
    blocks = block_list(cols)
    opening = len(rows_in) == 1
    live = streamed(held, blocks)
    sources_at = sorted(set(live) | {save[0] for save in saves})

    def kernel(*refs):
        refs = list(refs)
        rows_refs = [refs.pop(0) for _ in rows_in]
        stays = {i: (refs.pop(0), held[i][2], held[i][1], True) for i in held}
        sources = {i: refs.pop(0) for i in sources_at}
        exact, rounded = refs.pop(0), refs.pop(0)
        for i, _, units in saves:
            stays[i] = (refs.pop(0), len(block_list(units)), 0, False)
        x_all, dy_all = (refs.pop(0), refs.pop(0)) if opening else rows_refs
        slots = {i: refs.pop(0) for i in live}
        sems = refs.pop(0)
        stream = Stream(sources, slots, sems, base, blocks, stays)
        stream.open()
        if opening:
            spread(rows_refs[0], x_all, dy_all, counts)
        for step, (at, width) in enumerate(blocks):
            for i in range(3):
                weight = stream.take(i, step)[...]
                if i < 2:
                    part = dot(x_all[...], weight)
                else:
                    part = dot(dy_all[...], weight, NT)
                here = slice(i * cols + at, i * cols + at + width)
                exact[:, here] = part
                rounded[:, here] = part.astype(jnp.bfloat16)
                stream.done(i, step)

    shapes = [
        jax.ShapeDtypeStruct((rows, 3 * cols), jnp.float32),
        jax.ShapeDtypeStruct((rows, 3 * cols), jnp.bfloat16),
    ]
    shapes += [jax.ShapeDtypeStruct((wide, units), jnp.bfloat16) for _, _, units in saves]
    if opening:
        shapes += [jax.ShapeDtypeStruct((rows, wide), jnp.bfloat16)] * 2
    scratch = stream_scratch(wide, live)
    return pl.pallas_call(
        kernel,
        in_specs=[VMEM] * (len(rows_in) + len(held)) + [ANY] * len(sources_at),
        out_specs=[VMEM] * len(shapes),
        out_shape=shapes,
        scratch_shapes=scratch,
        compiler_params=params(6 * len(live) + 8),
        cost_estimate=cost(6 * 256 * wide * cols, 6 * wide * cols),
        name="first_phase",
    )(*rows_in, *[held[i][0] for i in held], *[weights[i] for i in sources_at])


def second_phase(parts, sums, weights, held, base, cols, counts, last):
    wide = weights[0].shape[0]
    rows = counts[0] * CAP
    feat = wide // counts[1]
    slabs = counts[0] * counts[1] * SLAB
    blocks = block_list(cols)
    live = streamed(held, blocks)
    order = (1, 0, 2) if 1 in held else (0, 1, 2)

    def kernel(*refs):
        refs = list(refs)
        part_refs = [refs.pop(0) for _ in parts]
        sum_refs = [refs.pop(0) for _ in sums]
        stays = {i: (refs.pop(0), held[i][2], held[i][1], True) for i in held}
        sources = {i: refs.pop(0) for i in live}
        hidden = refs.pop(0)
        outs = [refs.pop(0) for _ in range(1 if last else 2)]
        slots = {i: refs.pop(0) for i in live}
        sems, gate_grad, up_grad, *rest = refs
        acc = rest[:2] if last else outs
        stream = Stream(sources, slots, sems, base, blocks, stays)
        stream.open()
        for at, width in blocks:
            gate, up, hidden_grad = [
                sum(p[:, i * cols + at : i * cols + at + width].astype(jnp.float32) for p in part_refs)
                for i in range(3)
            ]
            sig = 1.0 / (1.0 + jnp.exp(-gate))
            act = gate * sig
            here = slice(at, at + width)
            hidden[:, here] = (act * up).astype(jnp.bfloat16)
            gate_grad[:, here] = (
                hidden_grad * up * sig * (1.0 + gate * (1.0 - sig))
            ).astype(jnp.bfloat16)
            up_grad[:, here] = (hidden_grad * act).astype(jnp.bfloat16)
        if last:
            packed = rest[2]
            packed[...] = jnp.zeros_like(packed)
        filled = [False, False]
        for step, (at, width) in enumerate(blocks):
            here = slice(at, at + width)
            for i in order:
                weight = stream.take(i, step)[...]
                left = (gate_grad, up_grad, hidden)[i]
                part = dot(left[:, here], weight, NN if i == 2 else NT)
                which = 0 if i == 2 else 1
                if filled[which]:
                    acc[which][...] += part
                elif sums:
                    acc[which][...] = sum_refs[which][...] + part
                else:
                    acc[which][...] = part
                filled[which] = True
                stream.done(i, step)
        if last:
            for device in range(counts[0] * counts[1]):
                block, outer = device // counts[1], device % counts[1]
                for which in range(2):
                    to = device * SLAB + which * CAP
                    packed[to : to + CAP, :] = acc[which][
                        block * CAP : (block + 1) * CAP, outer * feat : (outer + 1) * feat
                    ]
            outs[0][...] = packed[...].astype(jnp.bfloat16)

    scratch = stream_scratch(wide, live)
    scratch += [pltpu.VMEM((rows, cols), jnp.bfloat16)] * 2
    shapes = [jax.ShapeDtypeStruct((rows, cols), jnp.bfloat16)]
    if last:
        scratch += [pltpu.VMEM((rows, wide), jnp.float32)] * 2
        scratch += [pltpu.VMEM((slabs, feat), jnp.float32)]
        shapes += [jax.ShapeDtypeStruct((slabs, feat), jnp.bfloat16)]
    else:
        shapes += [jax.ShapeDtypeStruct((rows, wide), jnp.float32)] * 2
    return pl.pallas_call(
        kernel,
        in_specs=[VMEM] * (len(parts) + len(sums) + len(held)) + [ANY] * len(live),
        out_specs=[VMEM] * len(shapes),
        out_shape=shapes,
        scratch_shapes=scratch,
        compiler_params=params(6 * len(live) + 10),
        cost_estimate=cost(6 * 256 * wide * cols, 6 * wide * cols),
        name="second_phase",
    )(*parts, *sums, *[held[i][0] for i in held], *[weights[i] for i in live])


def outer_products(hiddens, dy_all, blocks, shape, earlier):
    wide = shape[1]

    def kernel(*refs):
        hidden_refs, dy = refs[: len(hiddens)], refs[len(hiddens)]
        out, held, sems = refs[-3:]

        def copy(i):
            _, _, row, width = blocks[i]
            slot = held.at[i % DEPTH]
            source = slot if width == BLOCK else slot.at[pl.ds(0, width), :]
            return pltpu.make_async_copy(source, out.at[pl.ds(row, width), :], sems.at[i % DEPTH])

        for i, (chunk, at, _, width) in enumerate(blocks):
            if i >= DEPTH:
                copy(i - DEPTH).wait()
            left = hidden_refs[chunk][:, at : at + width]
            held[i % DEPTH, 0:width, :] = dot(left, dy[...], TN).astype(jnp.bfloat16)
            copy(i).start()
        for i in range(max(0, len(blocks) - DEPTH), len(blocks)):
            copy(i).wait()

    total = sum(block[3] for block in blocks)
    return pl.pallas_call(
        kernel,
        in_specs=[VMEM] * (len(hiddens) + 1) + [ANY] * len(earlier),
        out_specs=ANY,
        out_shape=jax.ShapeDtypeStruct(shape, jnp.bfloat16),
        input_output_aliases={len(hiddens) + 1: 0} if earlier else {},
        scratch_shapes=[
            pltpu.VMEM((DEPTH, BLOCK, wide), jnp.bfloat16),
            pltpu.SemaphoreType.DMA((DEPTH,)),
        ],
        compiler_params=params(),
        cost_estimate=cost(2 * 256 * wide * total, 2 * wide * total),
        name="outer_products",
    )(*hiddens, dy_all, *earlier)


def from_peers(value, axis):
    size = lax.axis_size(axis)
    return [
        lax.ppermute(value, axis, [(i, (i + hop) % size) for i in range(size)])
        for hop in range(1, size)
    ]


def per_device(tokens, cotangent, expert_ids, gate_weights, w_gate, w_up, w_down):
    expert_count = lax.axis_size("expert")
    outer_count = lax.axis_size("tpout")
    counts = (expert_count, outer_count)
    tok_rows, feat = tokens.shape
    unit_cols = w_gate.shape[1]
    send, home = route_rows(
        tokens, cotangent, expert_ids.T, gate_weights.T, expert_count * outer_count, unit_cols
    )

    def exchange(rows):
        cut = rows.reshape(expert_count * outer_count, SLAB, feat)
        return lax.all_to_all(cut, ROUTE_AXES, 0, 0, tiled=True).reshape(rows.shape)

    weights = (w_gate, w_up, w_down)
    first_cols = unit_cols * FIRST_SHARE // 32 // 256 * 256 if unit_cols >= 4 * BLOCK else 0
    chunks = [(0, first_cols)] if first_cols else []
    chunks += [(first_cols, unit_cols - first_cols)]
    keeps = [min(KEEP_BLOCKS * BLOCK, cols // BLOCK * BLOCK or cols) for _, cols in chunks]
    rows_in = (exchange(send),)
    firsts, saved = [], []
    for n, (base, cols) in enumerate(chunks):
        saves = [(0, base, keeps[n])]
        exact, rounded, *more = first_phase(
            rows_in, weights, {}, saves, base, cols, counts
        )
        for i, _, units in saves:
            saved.append({i: (more.pop(0), 0, len(block_list(units)))})
        if more:
            rows_in = tuple(more)
        if firsts:
            before, exact = lax.optimization_barrier((firsts[-1][0], exact))
            firsts[-1][0] = before
        firsts.append([exact, from_peers(rounded, "tpin")])
    dy_all = rows_in[1]
    blocks = [
        (i, at, base + at, width)
        for i, (base, cols) in enumerate(chunks)
        for at, width in block_list(cols)
    ]
    sums, hiddens, down_grad = (), [], ()
    for (base, cols), (exact, others), held in zip(chunks, firsts, saved):
        last = base + cols == unit_cols
        if hiddens:
            early, blocks = blocks[:EARLY_BLOCKS], blocks[EARLY_BLOCKS:]
            down_grad = (outer_products(hiddens, dy_all, early, w_down.shape, down_grad),)
            exact, sums, down_grad = lax.optimization_barrier((exact, tuple(sums), down_grad))
        mine = exact + sum(o.astype(jnp.float32) for o in others)
        parts = [mine] + from_peers(mine.astype(jnp.bfloat16), "dp")
        hidden, *sums = second_phase(
            parts, sums, weights, held, base, cols, counts, last
        )
        hiddens.append(hidden)
    back = exchange(sums[0])
    down_grad = outer_products(hiddens, dy_all, blocks, w_down.shape, down_grad)
    layer_out, token_grad = combine_rows(back, home, tok_rows)
    return layer_out, token_grad, down_grad


def solution(mesh):
    wide = P("expert", ("dp", "tpin", "tpout"))
    rows = P("expert", None)
    into = P(("dp", "tpin"), ("expert", "tpout"))
    out_of = P(("expert", "tpout"), ("dp", "tpin"))
    return jax.shard_map(
        per_device,
        mesh=mesh,
        in_specs=(wide, wide, rows, rows, into, into, out_of),
        out_specs=(wide, wide, out_of),
        check_vma=False,
    )
```

```python
import jax
import jax.numpy as jnp
from jax import lax
from jax.experimental import pallas as pl
from jax.experimental.pallas import tpu as pltpu
from jax.sharding import PartitionSpec as P

EXPERTS = 8
HID = 8192
CAP = 6
BLOCK = 512
DEPTH = 4
KEEP_BLOCKS = 4
FIRST_SHARE = 16
EARLY_BLOCKS = 3
SLAB = 16
ROUTE_AXES = ("expert", "tpout")

NN = (((1,), (0,)), ((), ()))
NT = (((1,), (1,)), ((), ()))
TN = (((0,), (0,)), ((), ()))
VMEM = pl.BlockSpec(memory_space=pltpu.VMEM)
ANY = pl.BlockSpec(memory_space=pltpu.HBM)


def dot(left, right, dims=NN, precision=None):
    return lax.dot_general(
        left, right, dims, preferred_element_type=jnp.float32, precision=precision
    )


def params(mib=16):
    return pltpu.CompilerParams(vmem_limit_bytes=mib << 20)


def cost(flops, nbytes):
    return pl.CostEstimate(flops=int(flops), bytes_accessed=int(nbytes), transcendentals=0)


def route_rows(both, routes, devices, unit_cols):
    tok_rows, feat = both.shape[0] // 2, both.shape[1]
    rows = devices * SLAB
    top = routes.shape[0] // 2

    def kernel(both_ref, routes_ref, send, home):
        row = lax.broadcasted_iota(jnp.int32, (rows, tok_rows), 0)
        j = row % SLAB
        want = (row // SLAB * unit_cols // HID).astype(jnp.float32)
        slot = jnp.where(j < 2 * CAP, j % CAP, -1)
        is_x = j < CAP
        earlier = lax.broadcasted_iota(jnp.int32, (tok_rows, tok_rows), 0)
        later = lax.broadcasted_iota(jnp.int32, (tok_rows, tok_rows), 1)
        before = jnp.where(earlier < later, 1.0, 0.0)
        hit = jnp.zeros((rows, tok_rows), jnp.float32)
        weight = jnp.zeros((rows, tok_rows), jnp.float32)
        for k in range(top):
            same = routes_ref[k : k + 1, :] == want
            hit += jnp.where(same, 1.0, 0.0)
            weight += jnp.where(same, routes_ref[top + k : top + k + 1, :], 0.0)
        rank = dot(hit, before)
        chosen = jnp.where(rank == slot.astype(jnp.float32), hit, 0.0)
        pick = chosen.astype(jnp.bfloat16)
        row_weight = jnp.sum(chosen * weight, axis=1, keepdims=True)
        home[...] = jnp.where(is_x, chosen * weight, chosen)
        x = dot(pick, both_ref[:tok_rows, :])
        dy = row_weight * dot(pick, both_ref[tok_rows:, :])
        send[...] = jnp.where(is_x[:, 0:1], x, dy).astype(jnp.bfloat16)

    return pl.pallas_call(
        kernel,
        in_specs=[VMEM] * 2,
        out_specs=[VMEM] * 2,
        out_shape=[
            jax.ShapeDtypeStruct((rows, feat), jnp.bfloat16),
            jax.ShapeDtypeStruct((rows, tok_rows), jnp.float32),
        ],
        compiler_params=params(8),
        cost_estimate=cost(2e10, 1 << 25),
        name="route_rows",
    )(both, routes)


def combine_rows(back, home, tok_rows):
    rows, feat = back.shape

    def kernel(b, h, out, grad):
        j = lax.broadcasted_iota(jnp.int32, h.shape, 0) % SLAB
        vals = b[...].astype(jnp.float32)
        for_out = jnp.where(j < CAP, h[...], 0.0)
        for_grad = jnp.where(j < CAP, 0.0, h[...])
        out[...] = dot(for_out, vals, TN, lax.Precision.HIGHEST).astype(jnp.bfloat16)
        grad[...] = dot(for_grad.astype(jnp.bfloat16), b[...], TN).astype(jnp.bfloat16)

    shape = jax.ShapeDtypeStruct((tok_rows, feat), jnp.bfloat16)
    return pl.pallas_call(
        kernel,
        in_specs=[VMEM] * 2,
        out_specs=[VMEM] * 2,
        out_shape=[shape, shape],
        compiler_params=params(),
        name="combine_rows",
    )(back, home)


def block_list(cols):
    return [(at, min(BLOCK, cols - at)) for at in range(0, cols, BLOCK)]


class Stream:
    def __init__(self, sources, slots, sems, base, blocks, stays):
        self.sources, self.slots, self.sems = sources, slots, sems
        self.base, self.blocks, self.stays = base, blocks, stays

    def place(self, which, step):
        at, width = self.blocks[step]
        ref, count, offset, _ = self.stays.get(which, (None, 0, 0, False))
        if step < count:
            return ref.at[:, pl.ds(offset + at, width)]
        slot = self.slots[which].at[step % DEPTH]
        if width == BLOCK:
            return slot
        return slot.at[pl.ds(0, width), :] if which == 2 else slot.at[:, pl.ds(0, width)]

    def copy(self, which, step):
        _, count, _, present = self.stays.get(which, (None, 0, 0, False))
        if present and step < count:
            return None
        at, width = self.blocks[step]
        at = pl.ds(self.base + at, width)
        source = self.sources[which]
        return pltpu.make_async_copy(
            source.at[at, :] if which == 2 else source.at[:, at],
            self.place(which, step),
            self.sems.at[which, step % DEPTH],
        )

    def start(self, which, step):
        copy = self.copy(which, step) if step < len(self.blocks) else None
        if copy is not None:
            copy.start()

    def open(self):
        for step in range(DEPTH):
            for which in range(3):
                self.start(which, step)

    def take(self, which, step):
        copy = self.copy(which, step)
        if copy is not None:
            copy.wait()
        return self.place(which, step)

    def done(self, which, step):
        self.start(which, step + DEPTH)


def stream_scratch(wide, weights):
    slots = [
        pltpu.VMEM((DEPTH, BLOCK, wide) if which == 2 else (DEPTH, wide, BLOCK), jnp.bfloat16)
        for which in weights
    ]
    return slots + [pltpu.SemaphoreType.DMA((3, DEPTH))]


def slab_rows(shape, slot_dim, part, outer, counts):
    slot = lax.broadcasted_iota(jnp.int32, shape, slot_dim)
    row = lax.broadcasted_iota(jnp.int32, shape, 1 - slot_dim)
    device = slot // CAP * counts[1] + outer
    place = device * SLAB + part * CAP + slot % CAP
    return jnp.where(row == place, 1.0, 0.0).astype(jnp.bfloat16)


def spread(recv, x_all, dy_all, counts):
    feat = recv.shape[1]
    for outer in range(counts[1]):
        for part, whole in enumerate((x_all, dy_all)):
            pick = slab_rows((whole.shape[0], recv.shape[0]), 0, part, outer, counts)
            whole[:, outer * feat : (outer + 1) * feat] = dot(pick, recv[...]).astype(jnp.bfloat16)


def streamed(held, blocks):
    return [i for i in range(3) if i not in held or held[i][2] < len(blocks)]


def first_phase(rows_in, weights, held, saves, base, cols, counts):
    wide = weights[0].shape[0]
    rows = counts[0] * CAP
    blocks = block_list(cols)
    opening = len(rows_in) == 1
    live = streamed(held, blocks)
    sources_at = sorted(set(live) | {save[0] for save in saves})

    def kernel(*refs):
        refs = list(refs)
        rows_refs = [refs.pop(0) for _ in rows_in]
        stays = {i: (refs.pop(0), held[i][2], held[i][1], True) for i in held}
        sources = {i: refs.pop(0) for i in sources_at}
        exact, rounded = refs.pop(0), refs.pop(0)
        for i, _, units in saves:
            stays[i] = (refs.pop(0), len(block_list(units)), 0, False)
        x_all, dy_all = (refs.pop(0), refs.pop(0)) if opening else rows_refs
        slots = {i: refs.pop(0) for i in live}
        sems = refs.pop(0)
        stream = Stream(sources, slots, sems, base, blocks, stays)
        stream.open()
        if opening:
            spread(rows_refs[0], x_all, dy_all, counts)
        for step, (at, width) in enumerate(blocks):
            for i in range(3):
                weight = stream.take(i, step)[...]
                if i < 2:
                    part = dot(x_all[...], weight)
                else:
                    part = dot(dy_all[...], weight, NT)
                here = slice(i * cols + at, i * cols + at + width)
                exact[:, here] = part
                rounded[:, here] = part.astype(jnp.bfloat16)
                stream.done(i, step)

    shapes = [
        jax.ShapeDtypeStruct((rows, 3 * cols), jnp.float32),
        jax.ShapeDtypeStruct((rows, 3 * cols), jnp.bfloat16),
    ]
    shapes += [jax.ShapeDtypeStruct((wide, units), jnp.bfloat16) for _, _, units in saves]
    if opening:
        shapes += [jax.ShapeDtypeStruct((rows, wide), jnp.bfloat16)] * 2
    scratch = stream_scratch(wide, live)
    return pl.pallas_call(
        kernel,
        in_specs=[VMEM] * (len(rows_in) + len(held)) + [ANY] * len(sources_at),
        out_specs=[VMEM] * len(shapes),
        out_shape=shapes,
        scratch_shapes=scratch,
        compiler_params=params(6 * len(live) + 8),
        cost_estimate=cost(6 * 256 * wide * cols, 6 * wide * cols),
        name="first_phase",
    )(*rows_in, *[held[i][0] for i in held], *[weights[i] for i in sources_at])


def second_phase(parts, sums, weights, held, base, cols, counts, last):
    wide = weights[0].shape[0]
    rows = counts[0] * CAP
    feat = wide // counts[1]
    slabs = counts[0] * counts[1] * SLAB
    blocks = block_list(cols)
    live = streamed(held, blocks)
    order = (1, 0, 2) if 1 in held else (0, 1, 2)

    def kernel(*refs):
        refs = list(refs)
        part_refs = [refs.pop(0) for _ in parts]
        sum_refs = [refs.pop(0) for _ in sums]
        stays = {i: (refs.pop(0), held[i][2], held[i][1], True) for i in held}
        sources = {i: refs.pop(0) for i in live}
        hidden = refs.pop(0)
        outs = [refs.pop(0) for _ in range(1 if last else 2)]
        slots = {i: refs.pop(0) for i in live}
        sems, gate_grad, up_grad, *rest = refs
        acc = rest[:2] if last else outs
        stream = Stream(sources, slots, sems, base, blocks, stays)
        stream.open()
        for at, width in blocks:
            gate, up, hidden_grad = [
                sum(p[:, i * cols + at : i * cols + at + width].astype(jnp.float32) for p in part_refs)
                for i in range(3)
            ]
            sig = 1.0 / (1.0 + jnp.exp(-gate))
            act = gate * sig
            here = slice(at, at + width)
            hidden[:, here] = (act * up).astype(jnp.bfloat16)
            gate_grad[:, here] = (
                hidden_grad * up * sig * (1.0 + gate * (1.0 - sig))
            ).astype(jnp.bfloat16)
            up_grad[:, here] = (hidden_grad * act).astype(jnp.bfloat16)
        if last:
            packed = rest[2]
            packed[...] = jnp.zeros_like(packed)
        filled = [False, False]
        for step, (at, width) in enumerate(blocks):
            here = slice(at, at + width)
            for i in order:
                weight = stream.take(i, step)[...]
                left = (gate_grad, up_grad, hidden)[i]
                part = dot(left[:, here], weight, NN if i == 2 else NT)
                which = 0 if i == 2 else 1
                if filled[which]:
                    acc[which][...] += part
                elif sums:
                    acc[which][...] = sum_refs[which][...] + part
                else:
                    acc[which][...] = part
                filled[which] = True
                stream.done(i, step)
        if last:
            for device in range(counts[0] * counts[1]):
                block, outer = device // counts[1], device % counts[1]
                for which in range(2):
                    to = device * SLAB + which * CAP
                    packed[to : to + CAP, :] = acc[which][
                        block * CAP : (block + 1) * CAP, outer * feat : (outer + 1) * feat
                    ]
            outs[0][...] = packed[...].astype(jnp.bfloat16)

    scratch = stream_scratch(wide, live)
    scratch += [pltpu.VMEM((rows, cols), jnp.bfloat16)] * 2
    shapes = [jax.ShapeDtypeStruct((rows, cols), jnp.bfloat16)]
    if last:
        scratch += [pltpu.VMEM((rows, wide), jnp.float32)] * 2
        scratch += [pltpu.VMEM((slabs, feat), jnp.float32)]
        shapes += [jax.ShapeDtypeStruct((slabs, feat), jnp.bfloat16)]
    else:
        shapes += [jax.ShapeDtypeStruct((rows, wide), jnp.float32)] * 2
    return pl.pallas_call(
        kernel,
        in_specs=[VMEM] * (len(parts) + len(sums) + len(held)) + [ANY] * len(live),
        out_specs=[VMEM] * len(shapes),
        out_shape=shapes,
        scratch_shapes=scratch,
        compiler_params=params(6 * len(live) + 10),
        cost_estimate=cost(6 * 256 * wide * cols, 6 * wide * cols),
        name="second_phase",
    )(*parts, *sums, *[held[i][0] for i in held], *[weights[i] for i in live])


def outer_products(hiddens, dy_all, blocks, shape, earlier):
    wide = shape[1]

    def kernel(*refs):
        hidden_refs, dy = refs[: len(hiddens)], refs[len(hiddens)]
        out, held, sems = refs[-3:]

        def copy(i):
            _, _, row, width = blocks[i]
            slot = held.at[i % DEPTH]
            source = slot if width == BLOCK else slot.at[pl.ds(0, width), :]
            return pltpu.make_async_copy(source, out.at[pl.ds(row, width), :], sems.at[i % DEPTH])

        for i, (chunk, at, _, width) in enumerate(blocks):
            if i >= DEPTH:
                copy(i - DEPTH).wait()
            left = hidden_refs[chunk][:, at : at + width]
            held[i % DEPTH, 0:width, :] = dot(left, dy[...], TN).astype(jnp.bfloat16)
            copy(i).start()
        for i in range(max(0, len(blocks) - DEPTH), len(blocks)):
            copy(i).wait()

    total = sum(block[3] for block in blocks)
    return pl.pallas_call(
        kernel,
        in_specs=[VMEM] * (len(hiddens) + 1) + [ANY] * len(earlier),
        out_specs=ANY,
        out_shape=jax.ShapeDtypeStruct(shape, jnp.bfloat16),
        input_output_aliases={len(hiddens) + 1: 0} if earlier else {},
        scratch_shapes=[
            pltpu.VMEM((DEPTH, BLOCK, wide), jnp.bfloat16),
            pltpu.SemaphoreType.DMA((DEPTH,)),
        ],
        compiler_params=params(),
        cost_estimate=cost(2 * 256 * wide * total, 2 * wide * total),
        name="outer_products",
    )(*hiddens, dy_all, *earlier)


def from_peers(value, axis):
    size = lax.axis_size(axis)
    return [
        lax.ppermute(value, axis, [(i, (i + hop) % size) for i in range(size)])
        for hop in range(1, size)
    ]


def per_device(tokens, cotangent, expert_ids, gate_weights, w_gate, w_up, w_down):
    expert_count = lax.axis_size("expert")
    outer_count = lax.axis_size("tpout")
    counts = (expert_count, outer_count)
    tok_rows, feat = tokens.shape
    unit_cols = w_gate.shape[1]
    both = jnp.concatenate([tokens, cotangent], 0)
    routes = jnp.concatenate([expert_ids.T.astype(jnp.float32), gate_weights.T], 0)
    send, home = route_rows(both, routes, expert_count * outer_count, unit_cols)

    def exchange(rows):
        cut = rows.reshape(expert_count * outer_count, SLAB, feat)
        return lax.all_to_all(cut, ROUTE_AXES, 0, 0, tiled=True).reshape(rows.shape)

    weights = (w_gate, w_up, w_down)
    first_cols = unit_cols * FIRST_SHARE // 32 // 256 * 256 if unit_cols >= 4 * BLOCK else 0
    chunks = [(0, first_cols)] if first_cols else []
    chunks += [(first_cols, unit_cols - first_cols)]
    keeps = [min(KEEP_BLOCKS * BLOCK, cols // BLOCK * BLOCK or cols) for _, cols in chunks]
    rows_in = (exchange(send),)
    firsts, saved = [], []
    for n, (base, cols) in enumerate(chunks):
        if n == 0 and len(chunks) > 1:
            held, saves = {0: (w_gate, 0, len(block_list(cols)))}, [(1, base, keeps[n])]
        else:
            held, saves = {}, [(0, base, keeps[n])]
        exact, rounded, *more = first_phase(
            rows_in, weights, held, saves, base, cols, counts
        )
        for i, _, units in saves:
            saved.append({i: (more.pop(0), 0, len(block_list(units)))})
        if more:
            rows_in = tuple(more)
        if firsts:
            before, exact = lax.optimization_barrier((firsts[-1][0], exact))
            firsts[-1][0] = before
        firsts.append([exact, from_peers(rounded, "tpin")])
    dy_all = rows_in[1]
    blocks = [
        (i, at, base + at, width)
        for i, (base, cols) in enumerate(chunks)
        for at, width in block_list(cols)
    ]
    sums, hiddens, down_grad = (), [], ()
    for (base, cols), (exact, others), held in zip(chunks, firsts, saved):
        last = base + cols == unit_cols
        if hiddens:
            early, blocks = blocks[:EARLY_BLOCKS], blocks[EARLY_BLOCKS:]
            down_grad = (outer_products(hiddens, dy_all, early, w_down.shape, down_grad),)
            exact, sums, down_grad = lax.optimization_barrier((exact, tuple(sums), down_grad))
        mine = exact + sum(o.astype(jnp.float32) for o in others)
        parts = [mine] + from_peers(mine.astype(jnp.bfloat16), "dp")
        hidden, *sums = second_phase(
            parts, sums, weights, held, base, cols, counts, last
        )
        hiddens.append(hidden)
    back = exchange(sums[0])
    down_grad = outer_products(hiddens, dy_all, blocks, w_down.shape, down_grad)
    layer_out, token_grad = combine_rows(back, home, tok_rows)
    return layer_out, token_grad, down_grad


def solution(mesh):
    wide = P("expert", ("dp", "tpin", "tpout"))
    rows = P("expert", None)
    into = P(("dp", "tpin"), ("expert", "tpout"))
    out_of = P(("expert", "tpout"), ("dp", "tpin"))
    return jax.shard_map(
        per_device,
        mesh=mesh,
        in_specs=(wide, wide, rows, rows, into, into, out_of),
        out_specs=(wide, wide, out_of),
        check_vma=False,
    )
```

```python
import jax
import jax.numpy as jnp
from jax import lax
from jax.experimental import pallas as pl
from jax.experimental.pallas import tpu as pltpu
from jax.sharding import PartitionSpec as P

EXPERTS = 8
HID = 8192
CAP = 6
BLOCK = 512
DEPTH = 4
KEEP_BLOCKS = 4
FIRST_SHARE = 16
EARLY_BLOCKS = 3
SLAB = 16
ROUTE_AXES = ("expert", "tpout")

NN = (((1,), (0,)), ((), ()))
NT = (((1,), (1,)), ((), ()))
TN = (((0,), (0,)), ((), ()))
VMEM = pl.BlockSpec(memory_space=pltpu.VMEM)
ANY = pl.BlockSpec(memory_space=pltpu.HBM)


def dot(left, right, dims=NN, precision=None):
    return lax.dot_general(
        left, right, dims, preferred_element_type=jnp.float32, precision=precision
    )


def params(mib=16):
    return pltpu.CompilerParams(vmem_limit_bytes=mib << 20)


def cost(flops, nbytes):
    return pl.CostEstimate(flops=int(flops), bytes_accessed=int(nbytes), transcendentals=0)


def route_rows(both, routes, devices, unit_cols):
    tok_rows, feat = both.shape[0] // 2, both.shape[1]
    rows = devices * SLAB
    top = routes.shape[0] // 2

    def kernel(both_ref, routes_ref, send, home):
        row = lax.broadcasted_iota(jnp.int32, (rows, tok_rows), 0)
        j = row % SLAB
        want = (row // SLAB * unit_cols // HID).astype(jnp.float32)
        slot = jnp.where(j < 2 * CAP, j % CAP, -1)
        is_x = j < CAP
        earlier = lax.broadcasted_iota(jnp.int32, (tok_rows, tok_rows), 0)
        later = lax.broadcasted_iota(jnp.int32, (tok_rows, tok_rows), 1)
        before = jnp.where(earlier < later, 1.0, 0.0)
        hit = jnp.zeros((rows, tok_rows), jnp.float32)
        weight = jnp.zeros((rows, tok_rows), jnp.float32)
        for k in range(top):
            same = routes_ref[k : k + 1, :] == want
            hit += jnp.where(same, 1.0, 0.0)
            weight += jnp.where(same, routes_ref[top + k : top + k + 1, :], 0.0)
        rank = dot(hit, before)
        chosen = jnp.where(rank == slot.astype(jnp.float32), hit, 0.0)
        pick = chosen.astype(jnp.bfloat16)
        row_weight = jnp.sum(chosen * weight, axis=1, keepdims=True)
        home[...] = jnp.where(is_x, chosen * weight, chosen)
        x = dot(pick, both_ref[:tok_rows, :])
        dy = row_weight * dot(pick, both_ref[tok_rows:, :])
        send[...] = jnp.where(is_x[:, 0:1], x, dy).astype(jnp.bfloat16)

    return pl.pallas_call(
        kernel,
        in_specs=[VMEM] * 2,
        out_specs=[VMEM] * 2,
        out_shape=[
            jax.ShapeDtypeStruct((rows, feat), jnp.bfloat16),
            jax.ShapeDtypeStruct((rows, tok_rows), jnp.float32),
        ],
        compiler_params=params(8),
        cost_estimate=cost(2e10, 1 << 25),
        name="route_rows",
    )(both, routes)


def combine_rows(back, home, tok_rows):
    rows, feat = back.shape

    def kernel(b, h, out, grad):
        j = lax.broadcasted_iota(jnp.int32, h.shape, 0) % SLAB
        vals = b[...].astype(jnp.float32)
        for_out = jnp.where(j < CAP, h[...], 0.0)
        for_grad = jnp.where(j < CAP, 0.0, h[...])
        out[...] = dot(for_out, vals, TN, lax.Precision.HIGHEST).astype(jnp.bfloat16)
        grad[...] = dot(for_grad.astype(jnp.bfloat16), b[...], TN).astype(jnp.bfloat16)

    shape = jax.ShapeDtypeStruct((tok_rows, feat), jnp.bfloat16)
    return pl.pallas_call(
        kernel,
        in_specs=[VMEM] * 2,
        out_specs=[VMEM] * 2,
        out_shape=[shape, shape],
        compiler_params=params(),
        name="combine_rows",
    )(back, home)


def block_list(cols):
    return [(at, min(BLOCK, cols - at)) for at in range(0, cols, BLOCK)]


class Stream:
    def __init__(self, sources, slots, sems, base, blocks, stays):
        self.sources, self.slots, self.sems = sources, slots, sems
        self.base, self.blocks, self.stays = base, blocks, stays

    def place(self, which, step):
        at, width = self.blocks[step]
        ref, count, offset, _ = self.stays.get(which, (None, 0, 0, False))
        if step < count:
            return ref.at[:, pl.ds(offset + at, width)]
        slot = self.slots[which].at[step % DEPTH]
        if width == BLOCK:
            return slot
        return slot.at[pl.ds(0, width), :] if which == 2 else slot.at[:, pl.ds(0, width)]

    def copy(self, which, step):
        _, count, _, present = self.stays.get(which, (None, 0, 0, False))
        if present and step < count:
            return None
        at, width = self.blocks[step]
        at = pl.ds(self.base + at, width)
        source = self.sources[which]
        return pltpu.make_async_copy(
            source.at[at, :] if which == 2 else source.at[:, at],
            self.place(which, step),
            self.sems.at[which, step % DEPTH],
        )

    def start(self, which, step):
        copy = self.copy(which, step) if step < len(self.blocks) else None
        if copy is not None:
            copy.start()

    def open(self, order):
        for step in range(DEPTH):
            for which in order:
                self.start(which, step)

    def take(self, which, step):
        copy = self.copy(which, step)
        if copy is not None:
            copy.wait()
        return self.place(which, step)

    def done(self, which, step):
        self.start(which, step + DEPTH)


def stream_scratch(wide, weights):
    slots = [
        pltpu.VMEM((DEPTH, BLOCK, wide) if which == 2 else (DEPTH, wide, BLOCK), jnp.bfloat16)
        for which in weights
    ]
    return slots + [pltpu.SemaphoreType.DMA((3, DEPTH))]


def slab_rows(shape, slot_dim, part, outer, counts):
    slot = lax.broadcasted_iota(jnp.int32, shape, slot_dim)
    row = lax.broadcasted_iota(jnp.int32, shape, 1 - slot_dim)
    device = slot // CAP * counts[1] + outer
    place = device * SLAB + part * CAP + slot % CAP
    return jnp.where(row == place, 1.0, 0.0).astype(jnp.bfloat16)


def spread(recv, x_all, dy_all, counts):
    feat = recv.shape[1]
    for outer in range(counts[1]):
        for part, whole in enumerate((x_all, dy_all)):
            pick = slab_rows((whole.shape[0], recv.shape[0]), 0, part, outer, counts)
            whole[:, outer * feat : (outer + 1) * feat] = dot(pick, recv[...]).astype(jnp.bfloat16)


def streamed(held, blocks):
    return [i for i in range(3) if i not in held or held[i][2] < len(blocks)]


def first_phase(rows_in, weights, held, saves, base, cols, counts):
    wide = weights[0].shape[0]
    rows = counts[0] * CAP
    blocks = block_list(cols)
    opening = len(rows_in) == 1
    live = streamed(held, blocks)
    sources_at = sorted(set(live) | {save[0] for save in saves})

    def kernel(*refs):
        refs = list(refs)
        rows_refs = [refs.pop(0) for _ in rows_in]
        stays = {i: (refs.pop(0), held[i][2], held[i][1], True) for i in held}
        sources = {i: refs.pop(0) for i in sources_at}
        exact, rounded = refs.pop(0), refs.pop(0)
        for i, _, units in saves:
            stays[i] = (refs.pop(0), len(block_list(units)), 0, False)
        x_all, dy_all = (refs.pop(0), refs.pop(0)) if opening else rows_refs
        slots = {i: refs.pop(0) for i in live}
        sems = refs.pop(0)
        stream = Stream(sources, slots, sems, base, blocks, stays)
        order = (0, 2, 1)
        stream.open(order)
        if opening:
            spread(rows_refs[0], x_all, dy_all, counts)
        for step, (at, width) in enumerate(blocks):
            for i in order:
                weight = stream.take(i, step)[...]
                if i < 2:
                    part = dot(x_all[...], weight)
                else:
                    part = dot(dy_all[...], weight, NT)
                here = slice(i * cols + at, i * cols + at + width)
                exact[:, here] = part
                rounded[:, here] = part.astype(jnp.bfloat16)
                stream.done(i, step)

    shapes = [
        jax.ShapeDtypeStruct((rows, 3 * cols), jnp.float32),
        jax.ShapeDtypeStruct((rows, 3 * cols), jnp.bfloat16),
    ]
    shapes += [jax.ShapeDtypeStruct((wide, units), jnp.bfloat16) for _, _, units in saves]
    if opening:
        shapes += [jax.ShapeDtypeStruct((rows, wide), jnp.bfloat16)] * 2
    scratch = stream_scratch(wide, live)
    return pl.pallas_call(
        kernel,
        in_specs=[VMEM] * (len(rows_in) + len(held)) + [ANY] * len(sources_at),
        out_specs=[VMEM] * len(shapes),
        out_shape=shapes,
        scratch_shapes=scratch,
        compiler_params=params(6 * len(live) + 8),
        cost_estimate=cost(6 * 256 * wide * cols, 6 * wide * cols),
        name="first_phase",
    )(*rows_in, *[held[i][0] for i in held], *[weights[i] for i in sources_at])


def second_phase(parts, sums, weights, held, base, cols, counts, last):
    wide = weights[0].shape[0]
    rows = counts[0] * CAP
    feat = wide // counts[1]
    slabs = counts[0] * counts[1] * SLAB
    blocks = block_list(cols)
    live = streamed(held, blocks)
    order = (1, 0, 2) if 1 in held else (0, 1, 2)

    def kernel(*refs):
        refs = list(refs)
        part_refs = [refs.pop(0) for _ in parts]
        sum_refs = [refs.pop(0) for _ in sums]
        stays = {i: (refs.pop(0), held[i][2], held[i][1], True) for i in held}
        sources = {i: refs.pop(0) for i in live}
        hidden = refs.pop(0)
        outs = [refs.pop(0) for _ in range(1 if last else 2)]
        slots = {i: refs.pop(0) for i in live}
        sems, gate_grad, up_grad, *rest = refs
        acc = rest[:2] if last else outs
        stream = Stream(sources, slots, sems, base, blocks, stays)
        stream.open(order)
        for at, width in blocks:
            gate, up, hidden_grad = [
                sum(p[:, i * cols + at : i * cols + at + width].astype(jnp.float32) for p in part_refs)
                for i in range(3)
            ]
            sig = 1.0 / (1.0 + jnp.exp(-gate))
            act = gate * sig
            here = slice(at, at + width)
            hidden[:, here] = (act * up).astype(jnp.bfloat16)
            gate_grad[:, here] = (
                hidden_grad * up * sig * (1.0 + gate * (1.0 - sig))
            ).astype(jnp.bfloat16)
            up_grad[:, here] = (hidden_grad * act).astype(jnp.bfloat16)
        if last:
            packed = rest[2]
            packed[...] = jnp.zeros_like(packed)
        filled = [False, False]
        for step, (at, width) in enumerate(blocks):
            here = slice(at, at + width)
            for i in order:
                weight = stream.take(i, step)[...]
                left = (gate_grad, up_grad, hidden)[i]
                part = dot(left[:, here], weight, NN if i == 2 else NT)
                which = 0 if i == 2 else 1
                if filled[which]:
                    acc[which][...] += part
                elif sums:
                    acc[which][...] = sum_refs[which][...] + part
                else:
                    acc[which][...] = part
                filled[which] = True
                stream.done(i, step)
        if last:
            for device in range(counts[0] * counts[1]):
                block, outer = device // counts[1], device % counts[1]
                for which in range(2):
                    to = device * SLAB + which * CAP
                    packed[to : to + CAP, :] = acc[which][
                        block * CAP : (block + 1) * CAP, outer * feat : (outer + 1) * feat
                    ]
            outs[0][...] = packed[...].astype(jnp.bfloat16)

    scratch = stream_scratch(wide, live)
    scratch += [pltpu.VMEM((rows, cols), jnp.bfloat16)] * 2
    shapes = [jax.ShapeDtypeStruct((rows, cols), jnp.bfloat16)]
    if last:
        scratch += [pltpu.VMEM((rows, wide), jnp.float32)] * 2
        scratch += [pltpu.VMEM((slabs, feat), jnp.float32)]
        shapes += [jax.ShapeDtypeStruct((slabs, feat), jnp.bfloat16)]
    else:
        shapes += [jax.ShapeDtypeStruct((rows, wide), jnp.float32)] * 2
    return pl.pallas_call(
        kernel,
        in_specs=[VMEM] * (len(parts) + len(sums) + len(held)) + [ANY] * len(live),
        out_specs=[VMEM] * len(shapes),
        out_shape=shapes,
        scratch_shapes=scratch,
        compiler_params=params(6 * len(live) + 10),
        cost_estimate=cost(6 * 256 * wide * cols, 6 * wide * cols),
        name="second_phase",
    )(*parts, *sums, *[held[i][0] for i in held], *[weights[i] for i in live])


def outer_products(hiddens, dy_all, blocks, shape, earlier):
    wide = shape[1]

    def kernel(*refs):
        hidden_refs, dy = refs[: len(hiddens)], refs[len(hiddens)]
        out, held, sems = refs[-3:]

        def copy(i):
            _, _, row, width = blocks[i]
            slot = held.at[i % DEPTH]
            source = slot if width == BLOCK else slot.at[pl.ds(0, width), :]
            return pltpu.make_async_copy(source, out.at[pl.ds(row, width), :], sems.at[i % DEPTH])

        for i, (chunk, at, _, width) in enumerate(blocks):
            if i >= DEPTH:
                copy(i - DEPTH).wait()
            left = hidden_refs[chunk][:, at : at + width]
            held[i % DEPTH, 0:width, :] = dot(left, dy[...], TN).astype(jnp.bfloat16)
            copy(i).start()
        for i in range(max(0, len(blocks) - DEPTH), len(blocks)):
            copy(i).wait()

    total = sum(block[3] for block in blocks)
    return pl.pallas_call(
        kernel,
        in_specs=[VMEM] * (len(hiddens) + 1) + [ANY] * len(earlier),
        out_specs=ANY,
        out_shape=jax.ShapeDtypeStruct(shape, jnp.bfloat16),
        input_output_aliases={len(hiddens) + 1: 0} if earlier else {},
        scratch_shapes=[
            pltpu.VMEM((DEPTH, BLOCK, wide), jnp.bfloat16),
            pltpu.SemaphoreType.DMA((DEPTH,)),
        ],
        compiler_params=params(),
        cost_estimate=cost(2 * 256 * wide * total, 2 * wide * total),
        name="outer_products",
    )(*hiddens, dy_all, *earlier)


def from_peers(value, axis):
    size = lax.axis_size(axis)
    return [
        lax.ppermute(value, axis, [(i, (i + hop) % size) for i in range(size)])
        for hop in range(1, size)
    ]


def per_device(tokens, cotangent, expert_ids, gate_weights, w_gate, w_up, w_down):
    expert_count = lax.axis_size("expert")
    outer_count = lax.axis_size("tpout")
    counts = (expert_count, outer_count)
    tok_rows, feat = tokens.shape
    unit_cols = w_gate.shape[1]
    both = jnp.concatenate([tokens, cotangent], 0)
    routes = jnp.concatenate([expert_ids.T.astype(jnp.float32), gate_weights.T], 0)
    send, home = route_rows(both, routes, expert_count * outer_count, unit_cols)

    def exchange(rows):
        cut = rows.reshape(expert_count * outer_count, SLAB, feat)
        return lax.all_to_all(cut, ROUTE_AXES, 0, 0, tiled=True).reshape(rows.shape)

    weights = (w_gate, w_up, w_down)
    first_cols = unit_cols * FIRST_SHARE // 32 // 256 * 256 if unit_cols >= 4 * BLOCK else 0
    chunks = [(0, first_cols)] if first_cols else []
    chunks += [(first_cols, unit_cols - first_cols)]
    keeps = [min(KEEP_BLOCKS * BLOCK, cols // BLOCK * BLOCK or cols) for _, cols in chunks]
    rows_in = (exchange(send),)
    firsts, saved = [], []
    for n, (base, cols) in enumerate(chunks):
        if n == 0 and len(chunks) > 1:
            held, saves = {0: (w_gate, 0, len(block_list(cols)))}, [(1, base, keeps[n])]
        else:
            held, saves = {}, [(0, base, keeps[n])]
        exact, rounded, *more = first_phase(
            rows_in, weights, held, saves, base, cols, counts
        )
        for i, _, units in saves:
            saved.append({i: (more.pop(0), 0, len(block_list(units)))})
        if more:
            rows_in = tuple(more)
        if firsts:
            before, exact = lax.optimization_barrier((firsts[-1][0], exact))
            firsts[-1][0] = before
        firsts.append([exact, from_peers(rounded, "tpin")])
    dy_all = rows_in[1]
    blocks = [
        (i, at, base + at, width)
        for i, (base, cols) in enumerate(chunks)
        for at, width in block_list(cols)
    ]
    sums, hiddens, down_grad = (), [], ()
    for (base, cols), (exact, others), held in zip(chunks, firsts, saved):
        last = base + cols == unit_cols
        if hiddens:
            early, blocks = blocks[:EARLY_BLOCKS], blocks[EARLY_BLOCKS:]
            down_grad = (outer_products(hiddens, dy_all, early, w_down.shape, down_grad),)
            exact, sums, down_grad = lax.optimization_barrier((exact, tuple(sums), down_grad))
        mine = exact + sum(o.astype(jnp.float32) for o in others)
        parts = [mine] + from_peers(mine.astype(jnp.bfloat16), "dp")
        hidden, *sums = second_phase(
            parts, sums, weights, held, base, cols, counts, last
        )
        hiddens.append(hidden)
    back = exchange(sums[0])
    down_grad = outer_products(hiddens, dy_all, blocks, w_down.shape, down_grad)
    layer_out, token_grad = combine_rows(back, home, tok_rows)
    return layer_out, token_grad, down_grad


def solution(mesh):
    wide = P("expert", ("dp", "tpin", "tpout"))
    rows = P("expert", None)
    into = P(("dp", "tpin"), ("expert", "tpout"))
    out_of = P(("expert", "tpout"), ("dp", "tpin"))
    return jax.shard_map(
        per_device,
        mesh=mesh,
        in_specs=(wide, wide, rows, rows, into, into, out_of),
        out_specs=(wide, wide, out_of),
        check_vma=False,
    )
```
